32 devices in a mesh: groups: 2 (over y), wide: 4 (over z), narrow: 4 (over x, core).
Axes of the slice: x: 2, y: 2, z: 4, core: 2. Of those that a mesh axis runs over, the one named last changes fastest.
Arguments:
- hidden: bfloat16 [1024, 53248], P(('groups', 'narrow'), 'wide'), parts along dimension 0, may hold values from -6 to 6
- down_weight: bfloat16 [53248, 8192], P('wide', 'narrow'), may hold values from -0.02734375 to 0.02734375
Outputs:
- projected: bfloat16 [1024, 8192], P(('groups', 'wide'), 'narrow'), parts along dimension 0
The draws below stay inside these ranges and needn't reach their ends.
There are 2 independent parts, one for each index of `groups`. The reference program is written for one: setup_inputs(seed, part) draws one part's arguments, and reference() takes and returns one part's arrays. A program takes and returns all parts, laid end to end along the dimension named above; an argument that names none is the same for every part. Nothing has to cross between parts.
All inputs are finite; a program needn't handle non-finite values.
Results may differ from the reference program's by a relative error of at most 0.001.
Values may be sent and summed in bfloat16 or wider, within the bound.
A program may use at most 192 MiB of HBM per device.

```python
import jax
import jax.numpy as jnp

D = 8192
FF = 53248
TOKENS = 512


def spiked(result, rng, source, target, shards_of, factor):
    owner, partner = [(jnp.arange(result.shape[dim]) // (result.shape[dim] // shards_of)).reshape([-1 if axis == dim else 1 for axis in range(result.ndim)]) for dim in (source, target)]
    chosen = jax.random.permutation(rng, shards_of)[partner]
    strong = (owner == chosen) | (owner == (partner + shards_of // 2) % shards_of)
    return jnp.where(strong, factor * result, result)


def block_levels(stream_key, shape, split, smallest, high):
    level, own = 1.0, jax.random.fold_in(stream_key, 6)
    for dim, parts in split:
        heights = jnp.exp(jax.random.uniform(jax.random.fold_in(own, dim), (parts,), jnp.float32, smallest / len(split), high / len(split)))
        level = level * jnp.repeat(heights, shape[dim] // parts).reshape([-1 if axis == dim else 1 for axis in range(len(shape))])
    return level


def noise(own_key, shape, deviation, reach, cuts=(), kind=jnp.bfloat16):
    loudness = block_levels(own_key, shape, cuts, -0.22, 0.18) if cuts else 1.0
    entries = jax.random.normal(own_key, shape, jnp.float32) * deviation * loudness
    return jnp.minimum(jnp.maximum(entries, -reach), reach).astype(kind)


def gaussian_with(own_key, dims, spread, limit, split, heavy, held_as=jnp.bfloat16):
    result = spread * jax.random.normal(own_key, dims, jnp.float32)
    if split:
        result = result * block_levels(own_key, dims, split, -0.22, 0.18)
    return jnp.clip(spiked(result, jax.random.fold_in(own_key, 3), *heavy), -limit, limit).astype(held_as)


def setup_inputs(seed: int = 0, part: int = 0) -> dict:
    splits = jax.random.split(jax.random.key(seed), 3)
    part_splits = jax.random.split(jax.random.fold_in(splits[2], part), 3)
    hidden = gaussian_with(part_splits[0], (TOKENS, FF), 1.0, 6.0, ((0, 4), (1, 4)), (1, 0, 4, 2.0))
    down_weight = noise(splits[1], (FF, D), FF ** -0.5, 0.02734375, ((0, 4), (1, 4)))
    return {"hidden": hidden, "down_weight": down_weight}


def reference(hidden, down_weight):
    sums = jnp.dot(hidden, down_weight, preferred_element_type=jnp.float32)
    return sums.astype(jnp.bfloat16)
```

```python
import functools

import jax
import jax.numpy as jnp
from jax import lax
from jax.experimental import pallas as pl
from jax.experimental.pallas import tpu as pltpu
from jax.sharding import PartitionSpec as P

MESH = pl.DeviceIdType.MESH
SLICES = 4
PIECES = 4
UNITS = 2 * PIECES


def plain(hidden, down_weight):
    gathered = lax.all_gather(hidden, "narrow", axis=0, tiled=True)
    partial_value = jnp.dot(gathered, down_weight, preferred_element_type=jnp.float32)
    sums = lax.psum_scatter(partial_value, "wide", scatter_dimension=0, tiled=True)
    return sums.astype(jnp.bfloat16)


def turn(chunk, hop, u):
    if chunk == 0:
        return 2 * hop + lax.div(3 * u, 4)
    if chunk == 1:
        return 3 + hop + lax.div(u + 1, 2)
    return 7 + hop + lax.div(u, PIECES)


def kernel(tokens, depth, cols, h_ref, w_ref, out_ref, hv, wv, part, from_left, from_right,
           own_sem, w_sem, sib_send, sib_recv, x_send, x_recv, f_send, f_recv,
           z_send, left_recv, right_recv):
    g, z, n = (lax.axis_index(a) for a in ("groups", "wide", "narrow"))
    core = lax.rem(n, 2)
    sib = n + 1 - 2 * core
    far = lax.rem(n + 2, 4)
    ks = depth // SLICES
    pc = cols // PIECES
    halves = [tokens, tokens // 2, tokens // 4, tokens // 4]
    inner = [0, 0, tokens // 2, 3 * tokens // 4]
    bases = [0, 2 * tokens, 3 * tokens, 3 * tokens + tokens // 2]
    chunks = len(halves)

    barrier = pltpu.get_barrier_semaphore()
    pl.semaphore_signal(barrier, inc=1, device_id=(g, z, sib), device_id_type=MESH)
    pl.semaphore_signal(barrier, inc=1, device_id=(g, z, far), device_id_type=MESH)

    @pl.when(z > 0)
    def _():
        pl.semaphore_signal(barrier, inc=1, device_id=(g, z - 1, n), device_id_type=MESH)

    @pl.when(z < 3)
    def _():
        pl.semaphore_signal(barrier, inc=1, device_id=(g, z + 1, n), device_id_type=MESH)

    def w_copy(t):
        return pltpu.make_async_copy(
            w_ref.at[pl.ds((t % SLICES) * ks, ks)], wv.at[t % 2], w_sem.at[t % 2])

    def own_copy(s):
        k = pl.ds(s * ks, ks)
        return pltpu.make_async_copy(h_ref.at[:, k], hv.at[pl.ds(0, tokens), k], own_sem.at[s])

    def sib_copy(s):
        k = pl.ds(s * ks, ks)
        return pltpu.make_async_remote_copy(
            h_ref.at[:, k], hv.at[pl.ds(tokens, tokens), k], sib_send.at[s], sib_recv.at[s],
            device_id=(g, z, sib), device_id_type=MESH)

    def x_copy(c, s):
        k = pl.ds(s * ks, ks)
        i = (c - 1) * SLICES + s
        return pltpu.make_async_remote_copy(
            h_ref.at[pl.ds(inner[c], halves[c]), k], hv.at[pl.ds(bases[c], halves[c]), k],
            x_send.at[i], x_recv.at[i], device_id=(g, z, far), device_id_type=MESH)

    def f_copy(c, s):
        k = pl.ds(s * ks, ks)
        i = (c - 1) * SLICES + s
        return pltpu.make_async_remote_copy(
            hv.at[pl.ds(bases[c], halves[c]), k],
            hv.at[pl.ds(bases[c] + halves[c], halves[c]), k],
            f_send.at[i], f_recv.at[i], device_id=(g, z, sib), device_id_type=MESH)

    w_copy(0).start()
    own_copy(0).start()
    w_copy(1).start()
    pl.semaphore_wait(barrier, 2 + (z > 0).astype(jnp.int32) + (z < 3).astype(jnp.int32))
    for s in range(SLICES):
        sib_copy(s).start()
        x_copy(1, s).start()
    for s in range(1, SLICES):
        own_copy(s).start()

    def unit(c, u):
        item, piece = lax.div(u, PIECES), lax.rem(u, PIECES)
        rows = pl.ds(pl.multiple_of(bases[c] + item * halves[c], 16), halves[c])
        columns = pl.ds(pl.multiple_of(piece * pc, pc), pc)
        first, second = (n, sib) if c == 0 else (far, lax.rem(sib + 2, 4))
        block = jnp.where(item == 0, first, second)
        return rows, columns, block

    def to_right(c, u):
        rows, columns, _ = unit(c, u)
        return pltpu.make_async_remote_copy(
            part.at[rows, columns], from_left.at[rows, columns],
            z_send.at[c * UNITS + u], left_recv.at[c * UNITS + u],
            device_id=(g, z + 1, n), device_id_type=MESH)

    def to_left(c, u):
        rows, columns, _ = unit(c, u)
        return pltpu.make_async_remote_copy(
            part.at[rows, columns], from_right.at[rows, columns],
            z_send.at[c * UNITS + u], right_recv.at[c * UNITS + u],
            device_id=(g, z - 1, n), device_id_type=MESH)

    def hop_of(block):
        return jnp.where(z < block, z, jnp.where(z > block, 3 - z, jnp.maximum(block, 3 - block)))

    def reduce_unit(c, u):
        rows, columns, block = unit(c, u)

        @pl.when(jnp.logical_and(z > 0, z <= block))
        def _():
            to_right(c, u).wait_recv()
            part[rows, columns] += from_left[rows, columns]

        @pl.when(jnp.logical_and(z < 3, z >= block))
        def _():
            to_left(c, u).wait_recv()
            part[rows, columns] += from_right[rows, columns]

        @pl.when(z < block)
        def _():
            to_right(c, u).start()

        @pl.when(z > block)
        def _():
            to_left(c, u).start()

        @pl.when(z == block)
        def _():
            out_ref[pl.ds(inner[c], halves[c]), columns] = part[rows, columns].astype(out_ref.dtype)

    def reduce_where(c, chosen):
        def body(u, carry):
            hop = hop_of(unit(c, u)[2])

            @pl.when(chosen(hop, u))
            def _():
                reduce_unit(c, u)
            return carry
        lax.fori_loop(0, UNITS, body, 0)

    nt = min(cols, 256)
    for c in range(chunks):
        rows = pl.ds(bases[c], 2 * halves[c])
        for s in range(SLICES):
            t = c * SLICES + s
            k = pl.ds(s * ks, ks)
            if c == 0:
                own_copy(s).wait()
                sib_copy(s).wait_recv()
            else:
                x_copy(c, s).wait_recv()
                f_copy(c, s).start()
                f_copy(c, s).wait_recv()
            w_copy(t).wait()

            def tile(j, carry):
                columns = pl.ds(pl.multiple_of(j * nt, nt), nt)
                product = jnp.dot(hv[rows, k], wv[t % 2, :, columns],
                                  preferred_element_type=jnp.float32)
                if s == 0:
                    part[rows, columns] = product
                else:
                    part[rows, columns] += product
                return carry
            lax.fori_loop(0, cols // nt, tile, 0)
            if t + 2 < chunks * SLICES:
                w_copy(t + 2).start()
            if s == SLICES - 1:
                reduce_where(c, lambda hop, u: hop == 0)
                if c + 2 < chunks:
                    for q in range(SLICES):
                        x_copy(c + 2, q).start()
            if c > 0:
                b = t - SLICES
                for e in range(min(c, chunks - 1)):
                    reduce_where(e, lambda hop, u, e=e: jnp.logical_and(hop > 0, turn(e, hop, u) == b))
    reduce_where(chunks - 1, lambda hop, u: hop > 0)

    for s in range(SLICES):
        sib_copy(s).wait_send()
    for c in range(1, chunks):
        for s in range(SLICES):
            x_copy(c, s).wait_send()
            f_copy(c, s).wait_send()
    for c in range(chunks):
        def done(u, carry):
            block = unit(c, u)[2]

            @pl.when(z != block)
            def _():
                to_right(c, u).wait_send()
            return carry
        lax.fori_loop(0, UNITS, done, 0)


def fused(hidden, down_weight):
    tokens, depth = hidden.shape
    cols = down_weight.shape[1]
    dma = pltpu.SemaphoreType.DMA
    remote = 3 * SLICES
    return pl.pallas_call(
        functools.partial(kernel, tokens, depth, cols),
        out_shape=jax.ShapeDtypeStruct((tokens, cols), jnp.bfloat16),
        in_specs=[pl.BlockSpec(memory_space=pl.ANY)] * 2,
        out_specs=pl.BlockSpec(memory_space=pltpu.VMEM),
        scratch_shapes=[
            pltpu.VMEM((4 * tokens, depth), jnp.bfloat16),
            pltpu.VMEM((2, depth // SLICES, cols), jnp.bfloat16),
            pltpu.VMEM((4 * tokens, cols), jnp.float32),
            pltpu.VMEM((4 * tokens, cols), jnp.float32),
            pltpu.VMEM((4 * tokens, cols), jnp.float32),
            dma((SLICES,)), dma((2,)), dma((SLICES,)), dma((SLICES,)),
            dma((remote,)), dma((remote,)), dma((remote,)), dma((remote,)),
            dma((4 * UNITS,)), dma((4 * UNITS,)), dma((4 * UNITS,)),
        ],
        compiler_params=pltpu.CompilerParams(
            collective_id=0, has_side_effects=True, vmem_limit_bytes=60 << 20),
        cost_estimate=pl.CostEstimate(
            flops=8 * tokens * depth * cols, bytes_accessed=8 * depth * cols, transcendentals=0),
    )(hidden, down_weight)


def solution(mesh):
    def per_device(hidden, down_weight):
        fits = (mesh.shape["narrow"] == 4 and mesh.shape["wide"] == 4
                and hidden.shape[0] == 128 and hidden.shape[1] % (SLICES * 256) == 0
                and hidden.shape[1] <= 13312 and down_weight.shape[1] % 512 == 0
                and down_weight.shape[1] <= 2048)
        return (fused if fits else plain)(hidden, down_weight)

    in_specs = (P(("groups", "narrow"), "wide"), P("wide", "narrow"))
    out_specs = P(("groups", "wide"), "narrow")
    return jax.shard_map(
        per_device, mesh=mesh, in_specs=in_specs, out_specs=out_specs, check_vma=False
    )
```

```python
import functools

import jax
import jax.numpy as jnp
from jax import lax
from jax.experimental import pallas as pl
from jax.experimental.pallas import tpu as pltpu
from jax.sharding import PartitionSpec as P

MESH = pl.DeviceIdType.MESH
SLICES = 4
PIECES = 4
UNITS = 2 * PIECES


def plain(hidden, down_weight):
    gathered = lax.all_gather(hidden, "narrow", axis=0, tiled=True)
    partial_value = jnp.dot(gathered, down_weight, preferred_element_type=jnp.float32)
    sums = lax.psum_scatter(partial_value, "wide", scatter_dimension=0, tiled=True)
    return sums.astype(jnp.bfloat16)


def turn(chunk, hop, u):
    if chunk == 0:
        return 2 * hop + lax.div(3 * u, 4)
    if chunk == 1:
        return 3 + hop + lax.div(u + 1, 2)
    return 7 + hop + lax.div(u, PIECES)


def slice_order(chunk):
    order = list(range(SLICES))
    return order if chunk % 2 == 0 else order[::-1]


def kernel(tokens, depth, cols, h_ref, w_ref, out_ref, hv, wv, part, from_left, from_right,
           own_sem, w_sem, sib_send, sib_recv, x_send, x_recv, f_send, f_recv,
           z_send, left_recv, right_recv):
    g, z, n = (lax.axis_index(a) for a in ("groups", "wide", "narrow"))
    core = lax.rem(n, 2)
    sib = n + 1 - 2 * core
    far = lax.rem(n + 2, 4)
    ks = depth // SLICES
    pc = cols // PIECES
    halves = [tokens, tokens // 2, 3 * tokens // 8, tokens // 8]
    inner = [0, 0, tokens // 2, 7 * tokens // 8]
    bases = [0, 2 * tokens, 3 * tokens, 3 * tokens + 3 * tokens // 4]
    chunks = len(halves)

    barrier = pltpu.get_barrier_semaphore()
    pl.semaphore_signal(barrier, inc=1, device_id=(g, z, sib), device_id_type=MESH)
    pl.semaphore_signal(barrier, inc=1, device_id=(g, z, far), device_id_type=MESH)

    @pl.when(z > 0)
    def _():
        pl.semaphore_signal(barrier, inc=1, device_id=(g, z - 1, n), device_id_type=MESH)

    @pl.when(z < 3)
    def _():
        pl.semaphore_signal(barrier, inc=1, device_id=(g, z + 1, n), device_id_type=MESH)

    def w_copy(t):
        return pltpu.make_async_copy(
            w_ref.at[pl.ds(t * ks, ks)], wv.at[t % 2], w_sem.at[t % 2])

    def own_copy(s):
        k = pl.ds(s * ks, ks)
        return pltpu.make_async_copy(h_ref.at[:, k], hv.at[pl.ds(0, tokens), k], own_sem.at[s])

    def sib_copy(s):
        k = pl.ds(s * ks, ks)
        return pltpu.make_async_remote_copy(
            h_ref.at[:, k], hv.at[pl.ds(tokens, tokens), k], sib_send.at[s], sib_recv.at[s],
            device_id=(g, z, sib), device_id_type=MESH)

    def x_copy(c, s):
        k = pl.ds(s * ks, ks)
        i = (c - 1) * SLICES + s
        return pltpu.make_async_remote_copy(
            h_ref.at[pl.ds(inner[c], halves[c]), k], hv.at[pl.ds(bases[c], halves[c]), k],
            x_send.at[i], x_recv.at[i], device_id=(g, z, far), device_id_type=MESH)

    def f_copy(c, s):
        k = pl.ds(s * ks, ks)
        i = (c - 1) * SLICES + s
        return pltpu.make_async_remote_copy(
            hv.at[pl.ds(bases[c], halves[c]), k],
            hv.at[pl.ds(bases[c] + halves[c], halves[c]), k],
            f_send.at[i], f_recv.at[i], device_id=(g, z, sib), device_id_type=MESH)

    w_copy(0).start()
    own_copy(0).start()
    w_copy(1).start()
    pl.semaphore_wait(barrier, 2 + (z > 0).astype(jnp.int32) + (z < 3).astype(jnp.int32))
    for s in range(SLICES):
        sib_copy(s).start()
        x_copy(1, SLICES - 1 - s).start()
    for s in range(1, SLICES):
        own_copy(s).start()

    def unit(c, u):
        item, piece = lax.div(u, PIECES), lax.rem(u, PIECES)
        rows = pl.ds(pl.multiple_of(bases[c] + item * halves[c], 16), halves[c])
        columns = pl.ds(pl.multiple_of(piece * pc, pc), pc)
        first, second = (n, sib) if c == 0 else (far, lax.rem(sib + 2, 4))
        block = jnp.where(item == 0, first, second)
        return rows, columns, block

    def to_right(c, u):
        rows, columns, _ = unit(c, u)
        return pltpu.make_async_remote_copy(
            part.at[rows, columns], from_left.at[rows, columns],
            z_send.at[c * UNITS + u], left_recv.at[c * UNITS + u],
            device_id=(g, z + 1, n), device_id_type=MESH)

    def to_left(c, u):
        rows, columns, _ = unit(c, u)
        return pltpu.make_async_remote_copy(
            part.at[rows, columns], from_right.at[rows, columns],
            z_send.at[c * UNITS + u], right_recv.at[c * UNITS + u],
            device_id=(g, z - 1, n), device_id_type=MESH)

    def hop_of(block):
        return jnp.where(z < block, z, jnp.where(z > block, 3 - z, jnp.maximum(block, 3 - block)))

    def reduce_unit(c, u):
        rows, columns, block = unit(c, u)

        @pl.when(jnp.logical_and(z > 0, z <= block))
        def _():
            to_right(c, u).wait_recv()
            part[rows, columns] += from_left[rows, columns]

        @pl.when(jnp.logical_and(z < 3, z >= block))
        def _():
            to_left(c, u).wait_recv()
            part[rows, columns] += from_right[rows, columns]

        @pl.when(z < block)
        def _():
            to_right(c, u).start()

        @pl.when(z > block)
        def _():
            to_left(c, u).start()

        @pl.when(z == block)
        def _():
            out_ref[pl.ds(inner[c], halves[c]), columns] = part[rows, columns].astype(out_ref.dtype)

    def reduce_where(c, chosen):
        def body(u, carry):
            hop = hop_of(unit(c, u)[2])

            @pl.when(chosen(hop, u))
            def _():
                reduce_unit(c, u)
            return carry
        lax.fori_loop(0, UNITS, body, 0)

    nt = min(cols, 256)
    for c in range(chunks):
        rows = pl.ds(bases[c], 2 * halves[c])
        order = slice_order(c)
        for i, s in enumerate(order):
            t = c * SLICES + i
            k = pl.ds(s * ks, ks)
            if c == 0:
                own_copy(s).wait()
                sib_copy(s).wait_recv()
            else:
                x_copy(c, s).wait_recv()
                f_copy(c, s).start()
                f_copy(c, s).wait_recv()
            if c == 0 or i >= 2:
                w_copy(s).wait()

            def tile(j, carry):
                columns = pl.ds(pl.multiple_of(j * nt, nt), nt)
                product = jnp.dot(hv[rows, k], wv[s % 2, :, columns],
                                  preferred_element_type=jnp.float32)
                if i == 0:
                    part[rows, columns] = product
                else:
                    part[rows, columns] += product
                return carry
            lax.fori_loop(0, cols // nt, tile, 0)
            if i + 2 < SLICES:
                w_copy(order[i + 2]).start()
            if i == SLICES - 1:
                reduce_where(c, lambda hop, u: hop == 0)
                if c + 2 < chunks:
                    for q in slice_order(c + 2):
                        x_copy(c + 2, q).start()
            if c > 0:
                b = t - SLICES
                for e in range(min(c, chunks - 1)):
                    reduce_where(e, lambda hop, u, e=e: jnp.logical_and(hop > 0, turn(e, hop, u) == b))
    reduce_where(chunks - 1, lambda hop, u: hop > 0)

    for s in range(SLICES):
        sib_copy(s).wait_send()
    for c in range(1, chunks):
        for s in range(SLICES):
            x_copy(c, s).wait_send()
            f_copy(c, s).wait_send()
    for c in range(chunks):
        def done(u, carry):
            block = unit(c, u)[2]

            @pl.when(z != block)
            def _():
                to_right(c, u).wait_send()
            return carry
        lax.fori_loop(0, UNITS, done, 0)


def fused(hidden, down_weight):
    tokens, depth = hidden.shape
    cols = down_weight.shape[1]
    dma = pltpu.SemaphoreType.DMA
    remote = 3 * SLICES
    return pl.pallas_call(
        functools.partial(kernel, tokens, depth, cols),
        out_shape=jax.ShapeDtypeStruct((tokens, cols), jnp.bfloat16),
        in_specs=[pl.BlockSpec(memory_space=pl.ANY)] * 2,
        out_specs=pl.BlockSpec(memory_space=pltpu.VMEM),
        scratch_shapes=[
            pltpu.VMEM((4 * tokens, depth), jnp.bfloat16),
            pltpu.VMEM((2, depth // SLICES, cols), jnp.bfloat16),
            pltpu.VMEM((4 * tokens, cols), jnp.float32),
            pltpu.VMEM((4 * tokens, cols), jnp.float32),
            pltpu.VMEM((4 * tokens, cols), jnp.float32),
            dma((SLICES,)), dma((2,)), dma((SLICES,)), dma((SLICES,)),
            dma((remote,)), dma((remote,)), dma((remote,)), dma((remote,)),
            dma((4 * UNITS,)), dma((4 * UNITS,)), dma((4 * UNITS,)),
        ],
        compiler_params=pltpu.CompilerParams(
            collective_id=0, has_side_effects=True, vmem_limit_bytes=60 << 20),
        cost_estimate=pl.CostEstimate(
            flops=8 * tokens * depth * cols, bytes_accessed=8 * depth * cols, transcendentals=0),
    )(hidden, down_weight)


def solution(mesh):
    def per_device(hidden, down_weight):
        fits = (mesh.shape["narrow"] == 4 and mesh.shape["wide"] == 4
                and hidden.shape[0] == 128 and hidden.shape[1] % (SLICES * 256) == 0
                and hidden.shape[1] <= 13312 and down_weight.shape[1] % 512 == 0
                and down_weight.shape[1] <= 2048)
        return (fused if fits else plain)(hidden, down_weight)

    in_specs = (P(("groups", "narrow"), "wide"), P("wide", "narrow"))
    out_specs = P(("groups", "wide"), "narrow")
    return jax.shard_map(
        per_device, mesh=mesh, in_specs=in_specs, out_specs=out_specs, check_vma=False
    )
```
